32 devices in a mesh: grp: 2 (over x), gx: 16 (over z, y, core).
Axes of the slice: x: 2, y: 2, z: 4, core: 2. Of those that a mesh axis runs over, the one named last changes fastest.
Arguments:
- direction: float32 [64, 128, 128], P(('grp', 'gx')), parts along dimension 0, may hold values from -6 to 6
- kappa: float32 [64, 128, 128], P(('grp', 'gx')), parts along dimension 0, may hold values from 0.02 to 0.1
- velocity: float32 [3, 64, 128, 128], P(None, ('grp', 'gx')), parts along dimension 1, may hold values from -1 to 1
- prior_coef: float32 [64, 128, 128], P(('grp', 'gx')), parts along dimension 0, may hold values from 0.5 to 4
- noise_weight: float32 [4, 4096], P(None, ('grp', 'gx')), parts along dimension 1, may hold values from 1 to 10
- sensor_cell: int32 [4096], P(('grp', 'gx')), parts along dimension 0, may hold values from 0 to 32767
- sensor_slab: int32 [4096], P(('grp', 'gx')), parts along dimension 0, may hold values from 0 to 15
Outputs:
- hessian_action: float32 [64, 128, 128], P(('grp', 'gx')), parts along dimension 0
The draws below stay inside these ranges and needn't reach their ends.
There are 2 independent parts, one for each index of `grp`. The reference program is written for one: setup_inputs(seed, part) draws one part's arguments, and reference() takes and returns one part's arrays. A program takes and returns all parts, laid end to end along the dimension named above; each array names one. Nothing has to cross between parts.
All inputs are finite; a program needn't handle non-finite values.
Results may differ from the reference program's by a relative error of at most 0.00002.
Values sent between devices are 32-bit elements; how exact they have to be, the bound alone decides.
A program may use at most 64 MiB of HBM per device.

```python
import math
from functools import reduce
import jax
import jax.numpy as jnp

CX = 2
NY = 128
NZ = 128
STEPS = 4
NX = 32
NOBS = 2048
N_GX = 16


def plant(array, own_key, smallest, high):
    longest = array.shape.index(max(array.shape))
    spots = []
    for shift in (0, 1):
        where = [jax.random.randint(jax.random.fold_in(own_key, axis), (), 0, length) for axis, length in enumerate(array.shape)]
        where[longest] = (where[longest] + shift) % array.shape[longest]
        spots.append(tuple(where))
    return array.at[spots[0]].set(smallest).at[spots[1]].set(high)


def steps_of(stream_key, shape, split, low, high):
    level, own = 1.0, jax.random.fold_in(stream_key, 6)
    for axis_at, parts in split:
        draws = jnp.exp(jax.random.uniform(jax.random.fold_in(own, axis_at), (parts,), jnp.float32, low / len(split), high / len(split)))
        level = level * jnp.repeat(draws, shape[axis_at] // parts).reshape([-1 if axis == axis_at else 1 for axis in range(len(shape))])
    return level


def normal_values(rng, extent, spread, most, split=(), held_as=jnp.bfloat16):
    drawn = jax.random.normal(rng, extent, jnp.float32) * spread
    if len(split) > 0:
        drawn = steps_of(rng, extent, split, -0.22, 0.18) * drawn
    return jnp.clip(drawn, min=-most, max=most).astype(held_as)


def setup_inputs(seed: int = 0, part: int = 0) -> dict:
    seeds = jax.random.split(jax.random.key(seed), 8)
    part_splits = jax.random.split(jax.random.fold_in(seeds[7], part), 8)
    return {
        "direction": normal_values(part_splits[0], (NX, NY, NZ), 1.0, 6.0, ((0, 16),), jnp.float32),
        "kappa": jnp.clip(jnp.exp(math.log(0.1) - 1.609438 * jax.random.uniform(part_splits[1], (NX, NY, NZ), jnp.float32) ** steps_of(part_splits[1], (NX, NY, NZ), ((0, 16),), -0.2, 0.2)), 0.02, 0.1),
        "velocity": jnp.clip(jax.random.uniform(part_splits[2], (3, NX, NY, NZ), jnp.float32, -1.0, 1.0) * steps_of(part_splits[2], (3, NX, NY, NZ), ((1, 16),), -0.4, 0.0), -1.0, 1.0),
        "prior_coef": jnp.clip(jnp.exp(math.log(4.0) - 2.0794415 * jax.random.uniform(part_splits[3], (NX, NY, NZ), jnp.float32) ** steps_of(part_splits[3], (NX, NY, NZ), ((0, 16),), -0.2, 0.2)), 0.5, 4.0),
        "noise_weight": jnp.clip(jnp.exp(math.log(10.0) - 2.3025851 * jax.random.uniform(part_splits[4], (STEPS, NOBS), jnp.float32) ** steps_of(part_splits[4], (STEPS, NOBS), ((1, 16),), -0.2, 0.2)), 1.0, 10.0),
        "sensor_cell": plant(jax.random.randint(part_splits[5], (NOBS,), 0, CX * NY * NZ), jax.random.fold_in(part_splits[5], 1), 0, (CX * NY * NZ) - 1).astype(jnp.int32),
        "sensor_slab": plant(jax.random.randint(part_splits[6], (NOBS,), 0, N_GX), jax.random.fold_in(part_splits[6], 1), 0, N_GX - 1).astype(jnp.int32),
    }


time_step = 0.25
prior_scale = 0.01


def rate_terms(rates):
    kappa = rates[0]
    pieces = []
    for column in range(3):
        speed = rates[1 + column]
        pieces.append(time_step * (kappa + jax.nn.relu(-speed)))
        pieces.append(time_step * (kappa + jax.nn.relu(speed)))
    centre = 1.0 - reduce(lambda left, right: left + right, pieces)
    return [centre] + pieces


def shifted(values, dimension, offset):
    widths = [(0, 0), (0, 0), (0, 0)]
    widths[dimension] = (1, 1)
    padded = jnp.pad(values, widths)
    length = values.shape[dimension]
    return lax_slice(padded, dimension, 1 - offset, length)


def lax_slice(padded, dimension, begin, length):
    if dimension == 0:
        return padded[begin:begin + length]
    if dimension == 1:
        return padded[:, begin:begin + length]
    return padded[:, :, begin:begin + length]


def forward_global(field, terms):
    result = terms[0] * field
    for dimension in range(3):
        result = result + terms[1 + 2 * dimension] * shifted(field, dimension, -1)
        result = result + terms[2 + 2 * dimension] * shifted(field, dimension, 1)
    return result


def adjoint_global(field, terms):
    result = terms[0] * field
    for dimension in range(3):
        result = result + shifted(terms[1 + 2 * dimension] * field, dimension, 1)
        result = result + shifted(terms[2 + 2 * dimension] * field, dimension, -1)
    return result


def prior_global(field, coef):
    result = (coef + 6.0) * field
    for dimension in range(3):
        result = result - shifted(field, dimension, 1) - shifted(field, dimension, -1)
    return result


def reference(direction, kappa, velocity, prior_coef, noise_weight, sensor_cell, sensor_slab):
    slab_cells = CX * NY * NZ
    flat_index = (sensor_slab * slab_cells + sensor_cell).astype(jnp.int32)
    terms = rate_terms(jnp.concatenate([kappa[None], velocity], 0))
    state = direction
    weighted = []
    for step in range(STEPS):
        state = forward_global(state, terms)
        weighted.append(noise_weight[step] * state.reshape(-1)[flat_index])
    adjoint_field = jnp.zeros_like(direction)
    for step in reversed(range(STEPS)):
        adjoint_field = adjoint_field.reshape(-1).at[flat_index].add(weighted[step]).reshape(direction.shape)
        adjoint_field = adjoint_global(adjoint_field, terms)
    smooth = prior_global(prior_global(direction, prior_coef), prior_coef)
    return adjoint_field + prior_scale * smooth
```

```python
import functools

import jax
import jax.numpy as jnp
from jax import lax
from jax.experimental import pallas as pl
from jax.experimental.pallas import tpu as pltpu
from jax.sharding import PartitionSpec as P

STEPS = 4
CHUNKS = 2
GROUP = 16

time_step = 0.25
prior_scale = 0.01


def kernel(
    count,
    direction_hbm,
    kappa_hbm,
    velocity_hbm,
    prior_hbm,
    noise_ref,
    cell_ref,
    slab_ref,
    out_hbm,
    states,
    kappa,
    velocity,
    prior,
    centre,
    coef,
    pre,
    smooth,
    half,
    sends,
    halo_low,
    halo_high,
    tiles,
    row_hot,
    lane_hot,
    density,
    result,
    load_sem,
    out_sem,
    send_sem,
    recv_sem,
    tile_send,
    tile_recv,
):
    me = lax.axis_index("gx")
    planes, rows, lanes = pre.shape
    last = planes - 1
    chunk = rows // CHUNKS
    owned = noise_ref.shape[1]
    high = lax.rem(me + 1, count)
    low = lax.rem(me + count - 1, count)

    loads = [
        pltpu.make_async_copy(direction_hbm, states.at[0], load_sem.at[0]),
        pltpu.make_async_copy(kappa_hbm, kappa, load_sem.at[1]),
        pltpu.make_async_copy(velocity_hbm, velocity, load_sem.at[2]),
        pltpu.make_async_copy(prior_hbm, prior, load_sem.at[3]),
    ]
    for load in loads:
        load.start()

    barrier = pltpu.get_barrier_semaphore()

    def greet(offset, carry):
        pl.semaphore_signal(
            barrier,
            inc=1,
            device_id={"gx": lax.rem(me + offset, count)},
            device_id_type=pl.DeviceIdType.MESH,
        )
        return carry

    lax.fori_loop(1, count, greet, 0)

    tiles[me, 0:STEPS, :] = noise_ref[...]
    tiles[me, STEPS : STEPS + 1, :] = cell_ref[...].astype(jnp.float32)
    tiles[me, STEPS + 1 : STEPS + 2, :] = slab_ref[...].astype(jnp.float32)
    tiles[me, STEPS + 2 :, :] = jnp.zeros((tiles.shape[1] - STEPS - 2, owned), jnp.float32)

    @pl.when(me == 0)
    def _():
        halo_low[...] = jnp.zeros_like(halo_low)

    @pl.when(me == count - 1)
    def _():
        halo_high[...] = jnp.zeros_like(halo_high)

    def span(part):
        return pl.ds(part * chunk, chunk)

    def to_high(source, slot, part):
        return pltpu.make_async_remote_copy(
            src_ref=source.at[span(part)],
            dst_ref=halo_low.at[slot, span(part)],
            send_sem=send_sem.at[0, slot, part],
            recv_sem=recv_sem.at[0, slot, part],
            device_id={"gx": high},
            device_id_type=pl.DeviceIdType.MESH,
        )

    def to_low(source, slot, part):
        return pltpu.make_async_remote_copy(
            src_ref=source.at[span(part)],
            dst_ref=halo_high.at[slot, span(part)],
            send_sem=send_sem.at[1, slot, part],
            recv_sem=recv_sem.at[1, slot, part],
            device_id={"gx": low},
            device_id_type=pl.DeviceIdType.MESH,
        )

    started = []

    def send(top, bottom, slot, part):
        started.append((top, bottom, slot, part))

        @pl.when(me < count - 1)
        def _():
            to_high(top, slot, part).start()

        @pl.when(me > 0)
        def _():
            to_low(bottom, slot, part).start()

    def arrive(slot, part):
        @pl.when(me > 0)
        def _():
            to_high(states.at[0, 0], slot, part).wait_recv()

        @pl.when(me < count - 1)
        def _():
            to_low(states.at[0, 0], slot, part).wait_recv()

    pl.semaphore_wait(barrier, count - 1)
    loads[0].wait()
    for part in range(CHUNKS):
        send(states.at[0, last], states.at[0, 0], 0, part)

    def tile_copy(offset, source):
        return pltpu.make_async_remote_copy(
            src_ref=tiles.at[source],
            dst_ref=tiles.at[source],
            send_sem=tile_send.at[offset],
            recv_sem=tile_recv.at[offset],
            device_id={"gx": lax.rem(me + offset, count)},
            device_id_type=pl.DeviceIdType.MESH,
        )

    def tile_start(offset, carry):
        tile_copy(offset, me).start()
        return carry

    lax.fori_loop(1, count, tile_start, 0)

    row_at = lax.broadcasted_iota(jnp.int32, (rows, lanes), 0)
    lane_at = lax.broadcasted_iota(jnp.int32, (rows, lanes), 1)

    def next_row(value):
        return pltpu.roll(value, rows - 1, 0)

    def previous_row(value):
        return pltpu.roll(value, 1, 0)

    def next_lane(value):
        return pltpu.roll(value, lanes - 1, 1)

    def previous_lane(value):
        return pltpu.roll(value, 1, 1)

    loads[1].wait()
    loads[2].wait()
    for plane in range(planes):
        spread = kappa[plane]
        total = None
        edges = (None, None, row_at == rows - 1, row_at == 0, lane_at == lanes - 1, lane_at == 0)
        for column in range(3):
            speed = velocity[column, plane]
            for side in range(2):
                flow = jnp.maximum(-speed if side == 0 else speed, 0.0)
                piece = time_step * (spread + flow)
                total = piece if total is None else total + piece
                index = 2 * column + side
                edge = edges[index]
                coef[index, plane] = piece if edge is None else jnp.where(edge, 0.0, piece)
        centre[plane] = 1.0 - total

    def forward_local(step):
        for plane in range(planes):
            value = states[step, plane]
            result = centre[plane] * value
            if plane < last:
                result = result + coef[0, plane] * states[step, plane + 1]
            if plane > 0:
                result = result + coef[1, plane] * states[step, plane - 1]
            result = result + coef[2, plane] * next_row(value) + coef[3, plane] * previous_row(value)
            result = result + coef[4, plane] * next_lane(value) + coef[5, plane] * previous_lane(value)
            pre[plane] = result

    def prior_local(read, target, scale):
        for plane in range(planes):
            value = read(plane)
            result = (prior[plane] + 6.0) * value
            if plane < last:
                result = result - read(plane + 1)
            if plane > 0:
                result = result - read(plane - 1)
            result = result - jnp.where(row_at == rows - 1, 0.0, next_row(value))
            result = result - jnp.where(row_at == 0, 0.0, previous_row(value))
            result = result - jnp.where(lane_at == lanes - 1, 0.0, next_lane(value))
            result = result - jnp.where(lane_at == 0, 0.0, previous_lane(value))
            target[plane] = result

    prior_slot = 2 * STEPS
    cells_y = rows.bit_length() - 1

    def build_hot(first):
        def build(item, carry):
            tile = tiles.at[first + item]
            weight = tile[0:STEPS, :]
            cell = tile[STEPS : STEPS + 1, :].astype(jnp.int32)
            slab = tile[STEPS + 1 : STEPS + 2, :].astype(jnp.int32)
            row = jnp.where(slab == me, cell // lanes, -1)
            lane = cell % lanes
            at = pl.ds(pl.multiple_of(item * owned, owned), owned)
            tall = lax.broadcasted_iota(jnp.int32, (planes * rows, owned), 0)
            row_hot[:, at] = jnp.where(tall == row, 1.0, 0.0).astype(jnp.bfloat16)
            wide = lax.broadcasted_iota(jnp.int32, (lanes, owned), 0)
            here = wide == lane
            upper = weight.astype(jnp.bfloat16).astype(jnp.float32)
            lower = weight - upper
            for step in range(STEPS):
                lane_hot[step, 0:lanes, at] = jnp.where(here, upper[step : step + 1], 0.0).astype(jnp.bfloat16)
                lane_hot[step, lanes : 2 * lanes, at] = jnp.where(here, lower[step : step + 1], 0.0).astype(jnp.bfloat16)
            return carry

        lax.fori_loop(0, min(GROUP, count), build, 0)

    def add_density(step, first):
        both = lax.dot_general(
            row_hot[...],
            lane_hot[step],
            (((1,), (1,)), ((), ())),
            preferred_element_type=jnp.float32,
        )
        found = (both[:, :lanes] + both[:, lanes:]).reshape(planes, rows, lanes)
        if first:
            density[step] = found
        else:
            density[step] = density[step] + found

    def densities():
        build_hot(0)
        for step in range(STEPS):
            add_density(step, True)
        if count > GROUP:

            def more(block, carry):
                build_hot(block * GROUP)
                for step in range(STEPS):
                    add_density(step, False)
                return carry

            lax.fori_loop(1, count // GROUP, more, 0)

    for step in range(1, STEPS + 1):
        forward_local(step - 1)
        if step == 1:
            loads[3].wait()
            prior_local(lambda plane: states[0, plane], half, 1.0)
        if step == 2:
            half[0] = half[0] - halo_low[0]
            half[last] = half[last] - halo_high[0]
            for part in range(CHUNKS):
                send(half.at[last], half.at[0], prior_slot, part)
        if step == 3:

            def tile_wait(offset, carry):
                tile_copy(offset, me).wait_send()
                tile_copy(offset, lax.rem(me + count - offset, count)).wait_recv()
                return carry

            lax.fori_loop(1, count, tile_wait, 0)
            densities()
        if step == 4:
            prior_local(lambda plane: half[plane], smooth, 1.0)
        for part in range(CHUNKS):
            arrive(step - 1, part)
            at = span(part)
            for plane in range(planes):
                value = pre[plane, at]
                if plane == 0:
                    value = value + coef[1, 0, at] * halo_low[step - 1, at]
                if plane == last:
                    value = value + coef[0, last, at] * halo_high[step - 1, at]
                states[step, plane, at] = value
            if step < STEPS:
                send(states.at[step, last], states.at[step, 0], step, part)

    for order in range(STEPS):
        step = STEPS - order
        slot = STEPS + order
        for part in range(CHUNKS):
            at = span(part)
            if order > 0:
                arrive(slot - 1, part)
            for plane in range(planes):
                if order == 0:
                    value = density[step - 1, plane, at] * states[step, plane, at]
                else:
                    value = pre[plane, at]
                    if plane == 0:
                        value = value + halo_low[slot - 1, at]
                    if plane == last:
                        value = value + halo_high[slot - 1, at]
                result[plane, at] = value
                if plane == last:
                    sends[order, 0, at] = coef[0, last, at] * value
                if plane == 0:
                    sends[order, 1, at] = coef[1, 0, at] * value
            send(sends.at[order, 0], sends.at[order, 1], slot, part)
        for plane in range(planes):
            value = result[plane]
            total = centre[plane] * value
            if plane < last:
                total = total + coef[1, plane + 1] * result[plane + 1]
            if plane > 0:
                total = total + coef[0, plane - 1] * result[plane - 1]
            total = total + previous_row(coef[2, plane] * value) + next_row(coef[3, plane] * value)
            total = total + previous_lane(coef[4, plane] * value) + next_lane(coef[5, plane] * value)
            if step > 1:
                total = total + density[step - 2, plane] * states[step - 1, plane]
            else:
                total = total + prior_scale * smooth[plane]
            pre[plane] = total
        if order == 1:
            for part in range(CHUNKS):
                arrive(prior_slot, part)
            smooth[0] = smooth[0] - halo_low[prior_slot]
            smooth[last] = smooth[last] - halo_high[prior_slot]

    for part in range(CHUNKS):
        at = span(part)
        arrive(2 * STEPS - 1, part)
        for plane in range(planes):
            value = pre[plane, at]
            if plane == 0:
                value = value + halo_low[2 * STEPS - 1, at]
            if plane == last:
                value = value + halo_high[2 * STEPS - 1, at]
            result[plane, at] = value
    out = pltpu.make_async_copy(result, out_hbm, out_sem)
    out.start()

    @pl.when(me < count - 1)
    def _():
        for top, bottom, slot, part in started:
            to_high(top, slot, part).wait_send()

    @pl.when(me > 0)
    def _():
        for top, bottom, slot, part in started:
            to_low(bottom, slot, part).wait_send()

    out.wait()


def on_device(direction, kappa, velocity, prior_coef, noise_weight, sensor_cell, sensor_slab):
    count = lax.axis_size("gx")
    planes, rows, lanes = direction.shape
    owned = sensor_cell.shape[0]
    field = (planes, rows, lanes)
    slots = 2 * STEPS + 1
    group = min(GROUP, count) * owned
    hbm = pl.BlockSpec(memory_space=pl.ANY)
    vmem = pl.BlockSpec(memory_space=pltpu.VMEM)
    f32 = jnp.float32
    return pl.pallas_call(
        functools.partial(kernel, count),
        out_shape=jax.ShapeDtypeStruct(field, f32),
        in_specs=[hbm] * 4 + [vmem] * 3,
        out_specs=hbm,
        scratch_shapes=[
            pltpu.VMEM((STEPS + 1,) + field, f32),
            pltpu.VMEM(field, f32),
            pltpu.VMEM((3,) + field, f32),
            pltpu.VMEM(field, f32),
            pltpu.VMEM(field, f32),
            pltpu.VMEM((6,) + field, f32),
            pltpu.VMEM(field, f32),
            pltpu.VMEM(field, f32),
            pltpu.VMEM(field, f32),
            pltpu.VMEM((STEPS, 2, rows, lanes), f32),
            pltpu.VMEM((slots, rows, lanes), f32),
            pltpu.VMEM((slots, rows, lanes), f32),
            pltpu.VMEM((count, 8, owned), f32),
            pltpu.VMEM((planes * rows, group), jnp.bfloat16),
            pltpu.VMEM((STEPS, 2 * lanes, group), jnp.bfloat16),
            pltpu.VMEM((STEPS,) + field, f32),
            pltpu.VMEM(field, f32),
            pltpu.SemaphoreType.DMA((4,)),
            pltpu.SemaphoreType.DMA,
            pltpu.SemaphoreType.DMA((2, slots, CHUNKS)),
            pltpu.SemaphoreType.DMA((2, slots, CHUNKS)),
            pltpu.SemaphoreType.DMA((count,)),
            pltpu.SemaphoreType.DMA((count,)),
        ],
        compiler_params=pltpu.CompilerParams(
            collective_id=0, has_side_effects=True, vmem_limit_bytes=40 * 1024 * 1024
        ),
    )(
        direction,
        kappa,
        velocity,
        prior_coef,
        noise_weight,
        sensor_cell.reshape(1, owned),
        sensor_slab.reshape(1, owned),
    )


def solution(mesh):
    return jax.shard_map(
        on_device,
        mesh=mesh,
        in_specs=(
            P(("grp", "gx"), None, None),
            P(("grp", "gx"), None, None),
            P(None, ("grp", "gx"), None, None),
            P(("grp", "gx"), None, None),
            P(None, ("grp", "gx")),
            P(("grp", "gx")),
            P(("grp", "gx")),
        ),
        out_specs=P(("grp", "gx"), None, None),
        check_vma=False,
    )
```

```python
import functools

import jax
import jax.numpy as jnp
from jax import lax
from jax.experimental import pallas as pl
from jax.experimental.pallas import tpu as pltpu
from jax.sharding import PartitionSpec as P

STEPS = 4
CHUNKS = 2
GROUP = 16

time_step = 0.25
prior_scale = 0.01


def kernel(
    count,
    direction_hbm,
    kappa_hbm,
    velocity_hbm,
    prior_hbm,
    noise_hbm,
    cell_hbm,
    slab_hbm,
    out_hbm,
    states,
    kappa,
    velocity,
    prior,
    centre,
    coef,
    pre,
    smooth,
    half,
    sends,
    halo_low,
    halo_high,
    tiles,
    row_hot,
    lane_hot,
    density,
    result,
    noise_ref,
    cell_ref,
    slab_ref,
    load_sem,
    out_sem,
    send_sem,
    recv_sem,
    tile_send,
    tile_recv,
):
    me = lax.axis_index("gx")
    planes, rows, lanes = pre.shape
    last = planes - 1
    chunk = rows // CHUNKS
    owned = noise_ref.shape[1]
    high = lax.rem(me + 1, count)
    low = lax.rem(me + count - 1, count)

    loads = [
        pltpu.make_async_copy(noise_hbm, noise_ref, load_sem.at[4]),
        pltpu.make_async_copy(cell_hbm, cell_ref, load_sem.at[5]),
        pltpu.make_async_copy(slab_hbm, slab_ref, load_sem.at[6]),
        pltpu.make_async_copy(direction_hbm, states.at[0], load_sem.at[0]),
        pltpu.make_async_copy(kappa_hbm, kappa, load_sem.at[1]),
        pltpu.make_async_copy(velocity_hbm, velocity, load_sem.at[2]),
        pltpu.make_async_copy(prior_hbm, prior, load_sem.at[3]),
    ]
    for load in loads:
        load.start()

    barrier = pltpu.get_barrier_semaphore()

    def greet(offset, carry):
        pl.semaphore_signal(
            barrier,
            inc=1,
            device_id={"gx": lax.rem(me + offset, count)},
            device_id_type=pl.DeviceIdType.MESH,
        )
        return carry

    lax.fori_loop(1, count, greet, 0)

    for load in loads[:3]:
        load.wait()
    tiles[me, 0:STEPS, :] = noise_ref[...]
    tiles[me, STEPS : STEPS + 1, :] = cell_ref[...].astype(jnp.float32)
    tiles[me, STEPS + 1 : STEPS + 2, :] = slab_ref[...].astype(jnp.float32)
    tiles[me, STEPS + 2 :, :] = jnp.zeros((tiles.shape[1] - STEPS - 2, owned), jnp.float32)

    @pl.when(me == 0)
    def _():
        halo_low[...] = jnp.zeros_like(halo_low)

    @pl.when(me == count - 1)
    def _():
        halo_high[...] = jnp.zeros_like(halo_high)

    def span(part):
        return pl.ds(part * chunk, chunk)

    def to_high(source, slot, part):
        return pltpu.make_async_remote_copy(
            src_ref=source.at[span(part)],
            dst_ref=halo_low.at[slot, span(part)],
            send_sem=send_sem.at[0, slot, part],
            recv_sem=recv_sem.at[0, slot, part],
            device_id={"gx": high},
            device_id_type=pl.DeviceIdType.MESH,
        )

    def to_low(source, slot, part):
        return pltpu.make_async_remote_copy(
            src_ref=source.at[span(part)],
            dst_ref=halo_high.at[slot, span(part)],
            send_sem=send_sem.at[1, slot, part],
            recv_sem=recv_sem.at[1, slot, part],
            device_id={"gx": low},
            device_id_type=pl.DeviceIdType.MESH,
        )

    started = []

    def send(top, bottom, slot, part):
        started.append((top, bottom, slot, part))

        @pl.when(me < count - 1)
        def _():
            to_high(top, slot, part).start()

        @pl.when(me > 0)
        def _():
            to_low(bottom, slot, part).start()

    def arrive(slot, part):
        @pl.when(me > 0)
        def _():
            to_high(states.at[0, 0], slot, part).wait_recv()

        @pl.when(me < count - 1)
        def _():
            to_low(states.at[0, 0], slot, part).wait_recv()

    pl.semaphore_wait(barrier, count - 1)
    loads[3].wait()
    for part in range(CHUNKS):
        send(states.at[0, last], states.at[0, 0], 0, part)

    def tile_copy(offset, source):
        return pltpu.make_async_remote_copy(
            src_ref=tiles.at[source],
            dst_ref=tiles.at[source],
            send_sem=tile_send.at[offset],
            recv_sem=tile_recv.at[offset],
            device_id={"gx": lax.rem(me + offset, count)},
            device_id_type=pl.DeviceIdType.MESH,
        )

    def tile_start(offset, carry):
        tile_copy(offset, me).start()
        return carry

    lax.fori_loop(1, count, tile_start, 0)

    row_at = lax.broadcasted_iota(jnp.int32, (rows, lanes), 0)
    lane_at = lax.broadcasted_iota(jnp.int32, (rows, lanes), 1)

    def next_row(value):
        return pltpu.roll(value, rows - 1, 0)

    def previous_row(value):
        return pltpu.roll(value, 1, 0)

    def next_lane(value):
        return pltpu.roll(value, lanes - 1, 1)

    def previous_lane(value):
        return pltpu.roll(value, 1, 1)

    loads[4].wait()
    loads[5].wait()
    for plane in range(planes):
        spread = kappa[plane]
        total = None
        edges = (None, None, row_at == rows - 1, row_at == 0, lane_at == lanes - 1, lane_at == 0)
        for column in range(3):
            speed = velocity[column, plane]
            for side in range(2):
                flow = jnp.maximum(-speed if side == 0 else speed, 0.0)
                piece = time_step * (spread + flow)
                total = piece if total is None else total + piece
                index = 2 * column + side
                edge = edges[index]
                coef[index, plane] = piece if edge is None else jnp.where(edge, 0.0, piece)
        centre[plane] = 1.0 - total

    def forward_local(step):
        for plane in range(planes):
            value = states[step, plane]
            result = centre[plane] * value
            if plane < last:
                result = result + coef[0, plane] * states[step, plane + 1]
            if plane > 0:
                result = result + coef[1, plane] * states[step, plane - 1]
            result = result + coef[2, plane] * next_row(value) + coef[3, plane] * previous_row(value)
            result = result + coef[4, plane] * next_lane(value) + coef[5, plane] * previous_lane(value)
            pre[plane] = result

    def prior_local(read, target, scale):
        for plane in range(planes):
            value = read(plane)
            result = (prior[plane] + 6.0) * value
            if plane < last:
                result = result - read(plane + 1)
            if plane > 0:
                result = result - read(plane - 1)
            result = result - jnp.where(row_at == rows - 1, 0.0, next_row(value))
            result = result - jnp.where(row_at == 0, 0.0, previous_row(value))
            result = result - jnp.where(lane_at == lanes - 1, 0.0, next_lane(value))
            result = result - jnp.where(lane_at == 0, 0.0, previous_lane(value))
            target[plane] = result

    prior_slot = 2 * STEPS
    cells_y = rows.bit_length() - 1

    def build_hot(first):
        def build(item, carry):
            tile = tiles.at[first + item]
            weight = tile[0:STEPS, :]
            cell = tile[STEPS : STEPS + 1, :].astype(jnp.int32)
            slab = tile[STEPS + 1 : STEPS + 2, :].astype(jnp.int32)
            row = jnp.where(slab == me, cell // lanes, -1)
            lane = cell % lanes
            at = pl.ds(pl.multiple_of(item * owned, owned), owned)
            tall = lax.broadcasted_iota(jnp.int32, (planes * rows, owned), 0)
            row_hot[:, at] = jnp.where(tall == row, 1.0, 0.0).astype(jnp.bfloat16)
            wide = lax.broadcasted_iota(jnp.int32, (lanes, owned), 0)
            here = wide == lane
            upper = weight.astype(jnp.bfloat16).astype(jnp.float32)
            lower = weight - upper
            for step in range(STEPS):
                lane_hot[step, 0:lanes, at] = jnp.where(here, upper[step : step + 1], 0.0).astype(jnp.bfloat16)
                lane_hot[step, lanes : 2 * lanes, at] = jnp.where(here, lower[step : step + 1], 0.0).astype(jnp.bfloat16)
            return carry

        lax.fori_loop(0, min(GROUP, count), build, 0)

    def add_density(step, first):
        both = lax.dot_general(
            row_hot[...],
            lane_hot[step],
            (((1,), (1,)), ((), ())),
            preferred_element_type=jnp.float32,
        )
        found = (both[:, :lanes] + both[:, lanes:]).reshape(planes, rows, lanes)
        if first:
            density[step] = found
        else:
            density[step] = density[step] + found

    def densities():
        build_hot(0)
        for step in range(STEPS):
            add_density(step, True)
        if count > GROUP:

            def more(block, carry):
                build_hot(block * GROUP)
                for step in range(STEPS):
                    add_density(step, False)
                return carry

            lax.fori_loop(1, count // GROUP, more, 0)

    for step in range(1, STEPS + 1):
        forward_local(step - 1)
        if step == 1:
            loads[6].wait()
            prior_local(lambda plane: states[0, plane], half, 1.0)
        if step == 2:
            half[0] = half[0] - halo_low[0]
            half[last] = half[last] - halo_high[0]
            for part in range(CHUNKS):
                send(half.at[last], half.at[0], prior_slot, part)
        if step == 3:

            def tile_wait(offset, carry):
                tile_copy(offset, me).wait_send()
                tile_copy(offset, lax.rem(me + count - offset, count)).wait_recv()
                return carry

            lax.fori_loop(1, count, tile_wait, 0)
            densities()
        if step == 4:
            prior_local(lambda plane: half[plane], smooth, 1.0)
        for part in range(CHUNKS):
            arrive(step - 1, part)
            at = span(part)
            for plane in range(planes):
                value = pre[plane, at]
                if plane == 0:
                    value = value + coef[1, 0, at] * halo_low[step - 1, at]
                if plane == last:
                    value = value + coef[0, last, at] * halo_high[step - 1, at]
                states[step, plane, at] = value
            if step < STEPS:
                send(states.at[step, last], states.at[step, 0], step, part)

    for order in range(STEPS):
        step = STEPS - order
        slot = STEPS + order
        for part in range(CHUNKS):
            at = span(part)
            if order > 0:
                arrive(slot - 1, part)
            for plane in range(planes):
                if order == 0:
                    value = density[step - 1, plane, at] * states[step, plane, at]
                else:
                    value = pre[plane, at]
                    if plane == 0:
                        value = value + halo_low[slot - 1, at]
                    if plane == last:
                        value = value + halo_high[slot - 1, at]
                result[plane, at] = value
                if plane == last:
                    sends[order, 0, at] = coef[0, last, at] * value
                if plane == 0:
                    sends[order, 1, at] = coef[1, 0, at] * value
            send(sends.at[order, 0], sends.at[order, 1], slot, part)
        for plane in range(planes):
            value = result[plane]
            total = centre[plane] * value
            if plane < last:
                total = total + coef[1, plane + 1] * result[plane + 1]
            if plane > 0:
                total = total + coef[0, plane - 1] * result[plane - 1]
            total = total + previous_row(coef[2, plane] * value) + next_row(coef[3, plane] * value)
            total = total + previous_lane(coef[4, plane] * value) + next_lane(coef[5, plane] * value)
            if step > 1:
                total = total + density[step - 2, plane] * states[step - 1, plane]
            else:
                total = total + prior_scale * smooth[plane]
            pre[plane] = total
        if order == 1:
            for part in range(CHUNKS):
                arrive(prior_slot, part)
            smooth[0] = smooth[0] - halo_low[prior_slot]
            smooth[last] = smooth[last] - halo_high[prior_slot]

    for part in range(CHUNKS):
        at = span(part)
        arrive(2 * STEPS - 1, part)
        for plane in range(planes):
            value = pre[plane, at]
            if plane == 0:
                value = value + halo_low[2 * STEPS - 1, at]
            if plane == last:
                value = value + halo_high[2 * STEPS - 1, at]
            result[plane, at] = value
    out = pltpu.make_async_copy(result, out_hbm, out_sem)
    out.start()

    @pl.when(me < count - 1)
    def _():
        for top, bottom, slot, part in started:
            to_high(top, slot, part).wait_send()

    @pl.when(me > 0)
    def _():
        for top, bottom, slot, part in started:
            to_low(bottom, slot, part).wait_send()

    out.wait()


def on_device(direction, kappa, velocity, prior_coef, noise_weight, sensor_cell, sensor_slab):
    count = lax.axis_size("gx")
    planes, rows, lanes = direction.shape
    owned = sensor_cell.shape[0]
    field = (planes, rows, lanes)
    slots = 2 * STEPS + 1
    group = min(GROUP, count) * owned
    hbm = pl.BlockSpec(memory_space=pltpu.HBM)
    vmem = pl.BlockSpec(memory_space=pltpu.VMEM)
    f32 = jnp.float32
    return pl.pallas_call(
        functools.partial(kernel, count),
        out_shape=jax.ShapeDtypeStruct(field, f32),
        in_specs=[hbm] * 7,
        out_specs=hbm,
        scratch_shapes=[
            pltpu.VMEM((STEPS + 1,) + field, f32),
            pltpu.VMEM(field, f32),
            pltpu.VMEM((3,) + field, f32),
            pltpu.VMEM(field, f32),
            pltpu.VMEM(field, f32),
            pltpu.VMEM((6,) + field, f32),
            pltpu.VMEM(field, f32),
            pltpu.VMEM(field, f32),
            pltpu.VMEM(field, f32),
            pltpu.VMEM((STEPS, 2, rows, lanes), f32),
            pltpu.VMEM((slots, rows, lanes), f32),
            pltpu.VMEM((slots, rows, lanes), f32),
            pltpu.VMEM((count, 8, owned), f32),
            pltpu.VMEM((planes * rows, group), jnp.bfloat16),
            pltpu.VMEM((STEPS, 2 * lanes, group), jnp.bfloat16),
            pltpu.VMEM((STEPS,) + field, f32),
            pltpu.VMEM(field, f32),
            pltpu.VMEM((STEPS, owned), f32),
            pltpu.VMEM((1, owned), jnp.int32),
            pltpu.VMEM((1, owned), jnp.int32),
            pltpu.SemaphoreType.DMA((7,)),
            pltpu.SemaphoreType.DMA,
            pltpu.SemaphoreType.DMA((2, slots, CHUNKS)),
            pltpu.SemaphoreType.DMA((2, slots, CHUNKS)),
            pltpu.SemaphoreType.DMA((count,)),
            pltpu.SemaphoreType.DMA((count,)),
        ],
        compiler_params=pltpu.CompilerParams(
            collective_id=0, has_side_effects=True, vmem_limit_bytes=63 * 1024 * 1024
        ),
    )(
        direction,
        kappa,
        velocity,
        prior_coef,
        noise_weight,
        sensor_cell.reshape(1, owned),
        sensor_slab.reshape(1, owned),
    )


def solution(mesh):
    return jax.shard_map(
        on_device,
        mesh=mesh,
        in_specs=(
            P(("grp", "gx"), None, None),
            P(("grp", "gx"), None, None),
            P(None, ("grp", "gx"), None, None),
            P(("grp", "gx"), None, None),
            P(None, ("grp", "gx")),
            P(("grp", "gx")),
            P(("grp", "gx")),
        ),
        out_specs=P(("grp", "gx"), None, None),
        check_vma=False,
    )
```

```python
import functools

import jax
import jax.numpy as jnp
from jax import lax
from jax.experimental import pallas as pl
from jax.experimental.pallas import tpu as pltpu
from jax.sharding import PartitionSpec as P

STEPS = 4
CHUNKS = 2
GROUP = 16
RADIX = 4

time_step = 0.25
prior_scale = 0.01


def kernel(
    count,
    direction_hbm,
    kappa_hbm,
    velocity_hbm,
    prior_hbm,
    noise_hbm,
    cell_hbm,
    slab_hbm,
    out_hbm,
    states,
    kappa,
    velocity,
    prior,
    centre,
    coef,
    pre,
    smooth,
    half,
    sends,
    halo_low,
    halo_high,
    tiles,
    row_hot,
    lane_hot,
    density,
    result,
    noise_ref,
    cell_ref,
    slab_ref,
    load_sem,
    out_sem,
    send_sem,
    recv_sem,
    tile_send,
    tile_recv,
):
    me = lax.axis_index("gx")
    planes, rows, lanes = pre.shape
    last = planes - 1
    chunk = rows // CHUNKS
    owned = noise_ref.shape[1]
    high = lax.rem(me + 1, count)
    low = lax.rem(me + count - 1, count)

    loads = [
        pltpu.make_async_copy(noise_hbm, noise_ref, load_sem.at[4]),
        pltpu.make_async_copy(cell_hbm, cell_ref, load_sem.at[5]),
        pltpu.make_async_copy(slab_hbm, slab_ref, load_sem.at[6]),
        pltpu.make_async_copy(direction_hbm, states.at[0], load_sem.at[0]),
        pltpu.make_async_copy(kappa_hbm, kappa, load_sem.at[1]),
        pltpu.make_async_copy(velocity_hbm, velocity, load_sem.at[2]),
        pltpu.make_async_copy(prior_hbm, prior, load_sem.at[3]),
    ]
    for load in loads:
        load.start()

    barrier = pltpu.get_barrier_semaphore()

    def greet(target):
        pl.semaphore_signal(
            barrier, inc=1, device_id={"gx": target}, device_id_type=pl.DeviceIdType.MESH
        )

    @pl.when(me > 0)
    def _():
        greet(low)

    @pl.when(me < count - 1)
    def _():
        greet(high)

    rounds = gather_rounds(count)

    def member(stride, radix, offset):
        digit = lax.rem(me // stride, radix)
        return me + (lax.rem(digit + offset, radix) - digit) * stride

    greeted = jnp.where((me == 0) | (me == count - 1), 1, 2)
    for stride, radix in rounds:
        for offset in range(1, radix):
            greet(member(stride, radix, offset))
        greeted = greeted + radix - 1

    for load in loads[:3]:
        load.wait()
    tiles[me, 0:STEPS, :] = noise_ref[...]
    tiles[me, STEPS : STEPS + 1, :] = cell_ref[...].astype(jnp.float32)
    tiles[me, STEPS + 1 : STEPS + 2, :] = slab_ref[...].astype(jnp.float32)
    tiles[me, STEPS + 2 :, :] = jnp.zeros((tiles.shape[1] - STEPS - 2, owned), jnp.float32)

    @pl.when(me == 0)
    def _():
        halo_low[...] = jnp.zeros_like(halo_low)

    @pl.when(me == count - 1)
    def _():
        halo_high[...] = jnp.zeros_like(halo_high)

    def span(part):
        return pl.ds(part * chunk, chunk)

    def to_high(source, slot, part):
        return pltpu.make_async_remote_copy(
            src_ref=source.at[span(part)],
            dst_ref=halo_low.at[slot, span(part)],
            send_sem=send_sem.at[0, slot, part],
            recv_sem=recv_sem.at[0, slot, part],
            device_id={"gx": high},
            device_id_type=pl.DeviceIdType.MESH,
        )

    def to_low(source, slot, part):
        return pltpu.make_async_remote_copy(
            src_ref=source.at[span(part)],
            dst_ref=halo_high.at[slot, span(part)],
            send_sem=send_sem.at[1, slot, part],
            recv_sem=recv_sem.at[1, slot, part],
            device_id={"gx": low},
            device_id_type=pl.DeviceIdType.MESH,
        )

    started = []

    def send(top, bottom, slot, part):
        started.append((top, bottom, slot, part))

        @pl.when(me < count - 1)
        def _():
            to_high(top, slot, part).start()

        @pl.when(me > 0)
        def _():
            to_low(bottom, slot, part).start()

    def arrive(slot, part):
        @pl.when(me > 0)
        def _():
            to_high(states.at[0, 0], slot, part).wait_recv()

        @pl.when(me < count - 1)
        def _():
            to_low(states.at[0, 0], slot, part).wait_recv()

    pl.semaphore_wait(barrier, greeted)
    loads[3].wait()
    for part in range(CHUNKS):
        send(states.at[0, last], states.at[0, 0], 0, part)

    def tile_copy(turn, offset, source):
        stride, radix = rounds[turn]
        block = tiles.at[pl.ds((source // stride) * stride, stride)]
        return pltpu.make_async_remote_copy(
            src_ref=block,
            dst_ref=block,
            send_sem=tile_send.at[turn, offset],
            recv_sem=tile_recv.at[turn, offset],
            device_id={"gx": member(stride, radix, offset)},
            device_id_type=pl.DeviceIdType.MESH,
        )

    def tile_start(turn):
        for offset in range(1, rounds[turn][1]):
            tile_copy(turn, offset, me).start()

    def tile_finish(turn):
        stride, radix = rounds[turn]
        for offset in range(1, radix):
            tile_copy(turn, offset, me).wait_send()
            tile_copy(turn, offset, member(stride, radix, radix - offset)).wait_recv()

    tile_start(0)

    row_at = lax.broadcasted_iota(jnp.int32, (rows, lanes), 0)
    lane_at = lax.broadcasted_iota(jnp.int32, (rows, lanes), 1)

    def next_row(value):
        return pltpu.roll(value, rows - 1, 0)

    def previous_row(value):
        return pltpu.roll(value, 1, 0)

    def next_lane(value):
        return pltpu.roll(value, lanes - 1, 1)

    def previous_lane(value):
        return pltpu.roll(value, 1, 1)

    loads[4].wait()
    loads[5].wait()
    for plane in range(planes):
        spread = kappa[plane]
        total = None
        edges = (None, None, row_at == rows - 1, row_at == 0, lane_at == lanes - 1, lane_at == 0)
        for column in range(3):
            speed = velocity[column, plane]
            for side in range(2):
                flow = jnp.maximum(-speed if side == 0 else speed, 0.0)
                piece = time_step * (spread + flow)
                total = piece if total is None else total + piece
                index = 2 * column + side
                edge = edges[index]
                coef[index, plane] = piece if edge is None else jnp.where(edge, 0.0, piece)
        centre[plane] = 1.0 - total

    def forward_local(step):
        for plane in range(planes):
            value = states[step, plane]
            result = centre[plane] * value
            if plane < last:
                result = result + coef[0, plane] * states[step, plane + 1]
            if plane > 0:
                result = result + coef[1, plane] * states[step, plane - 1]
            result = result + coef[2, plane] * next_row(value) + coef[3, plane] * previous_row(value)
            result = result + coef[4, plane] * next_lane(value) + coef[5, plane] * previous_lane(value)
            pre[plane] = result

    def prior_local(read, target, scale):
        for plane in range(planes):
            value = read(plane)
            result = (prior[plane] + 6.0) * value
            if plane < last:
                result = result - read(plane + 1)
            if plane > 0:
                result = result - read(plane - 1)
            result = result - jnp.where(row_at == rows - 1, 0.0, next_row(value))
            result = result - jnp.where(row_at == 0, 0.0, previous_row(value))
            result = result - jnp.where(lane_at == lanes - 1, 0.0, next_lane(value))
            result = result - jnp.where(lane_at == 0, 0.0, previous_lane(value))
            target[plane] = result

    prior_slot = 2 * STEPS

    def build_hot(first):
        def build(item, carry):
            tile = tiles.at[first + item]
            weight = tile[0:STEPS, :]
            cell = tile[STEPS : STEPS + 1, :].astype(jnp.int32)
            slab = tile[STEPS + 1 : STEPS + 2, :].astype(jnp.int32)
            row = jnp.where(slab == me, cell // lanes, -1)
            lane = cell % lanes
            at = pl.ds(pl.multiple_of(item * owned, owned), owned)
            tall = lax.broadcasted_iota(jnp.int32, (planes * rows, owned), 0)
            row_hot[:, at] = jnp.where(tall == row, 1.0, 0.0).astype(jnp.bfloat16)
            wide = lax.broadcasted_iota(jnp.int32, (lanes, owned), 0)
            here = wide == lane
            upper = weight.astype(jnp.bfloat16).astype(jnp.float32)
            lower = weight - upper
            for step in range(STEPS):
                lane_hot[step, 0:lanes, at] = jnp.where(here, upper[step : step + 1], 0.0).astype(jnp.bfloat16)
                lane_hot[step, lanes : 2 * lanes, at] = jnp.where(here, lower[step : step + 1], 0.0).astype(jnp.bfloat16)
            return carry

        lax.fori_loop(0, min(GROUP, count), build, 0)

    def add_density(step, first):
        both = lax.dot_general(
            row_hot[...],
            lane_hot[step],
            (((1,), (1,)), ((), ())),
            preferred_element_type=jnp.float32,
        )
        found = (both[:, :lanes] + both[:, lanes:]).reshape(planes, rows, lanes)
        if first:
            density[step] = found
        else:
            density[step] = density[step] + found

    def densities():
        build_hot(0)
        for step in range(STEPS):
            add_density(step, True)
        if count > GROUP:

            def more(block, carry):
                build_hot(block * GROUP)
                for step in range(STEPS):
                    add_density(step, False)
                return carry

            lax.fori_loop(1, count // GROUP, more, 0)

    for step in range(1, STEPS + 1):
        forward_local(step - 1)
        if step == 1:
            loads[6].wait()
            prior_local(lambda plane: states[0, plane], half, 1.0)
        if step == 2:
            half[0] = half[0] - halo_low[0]
            half[last] = half[last] - halo_high[0]
            for part in range(CHUNKS):
                send(half.at[last], half.at[0], prior_slot, part)
        if step == 2:
            tile_finish(0)
            if len(rounds) > 1:
                tile_start(1)
        if step == 3:
            for turn in range(1, len(rounds)):
                tile_finish(turn)
                if turn + 1 < len(rounds):
                    tile_start(turn + 1)
            if count > GROUP:
                densities()
            else:
                build_hot(0)
        if step == 4 and count <= GROUP:
            add_density(STEPS - 1, True)
        if step == 4:
            prior_local(lambda plane: half[plane], smooth, 1.0)
        for part in range(CHUNKS):
            arrive(step - 1, part)
            at = span(part)
            for plane in range(planes):
                value = pre[plane, at]
                if plane == 0:
                    value = value + coef[1, 0, at] * halo_low[step - 1, at]
                if plane == last:
                    value = value + coef[0, last, at] * halo_high[step - 1, at]
                states[step, plane, at] = value
            if step < STEPS:
                send(states.at[step, last], states.at[step, 0], step, part)

    for order in range(STEPS):
        step = STEPS - order
        slot = STEPS + order
        for part in range(CHUNKS):
            at = span(part)
            if order > 0:
                arrive(slot - 1, part)
            for plane in range(planes):
                if order == 0:
                    value = density[step - 1, plane, at] * states[step, plane, at]
                else:
                    value = pre[plane, at]
                    if plane == 0:
                        value = value + halo_low[slot - 1, at]
                    if plane == last:
                        value = value + halo_high[slot - 1, at]
                result[plane, at] = value
                if plane == last:
                    sends[order, 0, at] = coef[0, last, at] * value
                if plane == 0:
                    sends[order, 1, at] = coef[1, 0, at] * value
            send(sends.at[order, 0], sends.at[order, 1], slot, part)
        if step > 1 and count <= GROUP:
            add_density(step - 2, True)
        for plane in range(planes):
            value = result[plane]
            total = centre[plane] * value
            if plane < last:
                total = total + coef[1, plane + 1] * result[plane + 1]
            if plane > 0:
                total = total + coef[0, plane - 1] * result[plane - 1]
            total = total + previous_row(coef[2, plane] * value) + next_row(coef[3, plane] * value)
            total = total + previous_lane(coef[4, plane] * value) + next_lane(coef[5, plane] * value)
            if step > 1:
                total = total + density[step - 2, plane] * states[step - 1, plane]
            else:
                total = total + prior_scale * smooth[plane]
            pre[plane] = total
        if order == 1:
            for part in range(CHUNKS):
                arrive(prior_slot, part)
            smooth[0] = smooth[0] - halo_low[prior_slot]
            smooth[last] = smooth[last] - halo_high[prior_slot]

    for part in range(CHUNKS):
        at = span(part)
        arrive(2 * STEPS - 1, part)
        for plane in range(planes):
            value = pre[plane, at]
            if plane == 0:
                value = value + halo_low[2 * STEPS - 1, at]
            if plane == last:
                value = value + halo_high[2 * STEPS - 1, at]
            result[plane, at] = value
    out = pltpu.make_async_copy(result, out_hbm, out_sem)
    out.start()

    @pl.when(me < count - 1)
    def _():
        for top, bottom, slot, part in started:
            to_high(top, slot, part).wait_send()

    @pl.when(me > 0)
    def _():
        for top, bottom, slot, part in started:
            to_low(bottom, slot, part).wait_send()

    out.wait()


def gather_rounds(count):
    rounds = []
    stride = 1
    while stride < count:
        radix = min(RADIX, count // stride)
        rounds.append((stride, radix))
        stride *= radix
    return rounds


def on_device(direction, kappa, velocity, prior_coef, noise_weight, sensor_cell, sensor_slab):
    count = lax.axis_size("gx")
    planes, rows, lanes = direction.shape
    owned = sensor_cell.shape[0]
    field = (planes, rows, lanes)
    slots = 2 * STEPS + 1
    group = min(GROUP, count) * owned
    hbm = pl.BlockSpec(memory_space=pltpu.HBM)
    vmem = pl.BlockSpec(memory_space=pltpu.VMEM)
    f32 = jnp.float32
    return pl.pallas_call(
        functools.partial(kernel, count),
        out_shape=jax.ShapeDtypeStruct(field, f32),
        in_specs=[hbm] * 7,
        out_specs=hbm,
        scratch_shapes=[
            pltpu.VMEM((STEPS + 1,) + field, f32),
            pltpu.VMEM(field, f32),
            pltpu.VMEM((3,) + field, f32),
            pltpu.VMEM(field, f32),
            pltpu.VMEM(field, f32),
            pltpu.VMEM((6,) + field, f32),
            pltpu.VMEM(field, f32),
            pltpu.VMEM(field, f32),
            pltpu.VMEM(field, f32),
            pltpu.VMEM((STEPS, 2, rows, lanes), f32),
            pltpu.VMEM((slots, rows, lanes), f32),
            pltpu.VMEM((slots, rows, lanes), f32),
            pltpu.VMEM((count, 8, owned), f32),
            pltpu.VMEM((planes * rows, group), jnp.bfloat16),
            pltpu.VMEM((STEPS, 2 * lanes, group), jnp.bfloat16),
            pltpu.VMEM((STEPS,) + field, f32),
            pltpu.VMEM(field, f32),
            pltpu.VMEM((STEPS, owned), f32),
            pltpu.VMEM((1, owned), jnp.int32),
            pltpu.VMEM((1, owned), jnp.int32),
            pltpu.SemaphoreType.DMA((7,)),
            pltpu.SemaphoreType.DMA,
            pltpu.SemaphoreType.DMA((2, slots, CHUNKS)),
            pltpu.SemaphoreType.DMA((2, slots, CHUNKS)),
            pltpu.SemaphoreType.DMA((len(gather_rounds(count)), RADIX)),
            pltpu.SemaphoreType.DMA((len(gather_rounds(count)), RADIX)),
        ],
        compiler_params=pltpu.CompilerParams(
            collective_id=0, has_side_effects=True, vmem_limit_bytes=63 * 1024 * 1024
        ),
    )(
        direction,
        kappa,
        velocity,
        prior_coef,
        noise_weight,
        sensor_cell.reshape(1, owned),
        sensor_slab.reshape(1, owned),
    )


def solution(mesh):
    return jax.shard_map(
        on_device,
        mesh=mesh,
        in_specs=(
            P(("grp", "gx"), None, None),
            P(("grp", "gx"), None, None),
            P(None, ("grp", "gx"), None, None),
            P(("grp", "gx"), None, None),
            P(None, ("grp", "gx")),
            P(("grp", "gx")),
            P(("grp", "gx")),
        ),
        out_specs=P(("grp", "gx"), None, None),
        check_vma=False,
    )
```

```python
import functools

import jax
import jax.numpy as jnp
from jax import lax
from jax.experimental import pallas as pl
from jax.experimental.pallas import tpu as pltpu
from jax.sharding import PartitionSpec as P

STEPS = 4
CHUNKS = 4
GROUP = 16
RADIX = 4

time_step = 0.25
prior_scale = 0.01


def kernel(
    count,
    direction_hbm,
    kappa_hbm,
    velocity_hbm,
    prior_hbm,
    noise_hbm,
    cell_hbm,
    slab_hbm,
    out_hbm,
    states,
    kappa,
    velocity,
    prior,
    centre,
    coef,
    pre,
    smooth,
    half,
    sends,
    halo_low,
    halo_high,
    tiles,
    row_hot,
    lane_hot,
    density,
    result,
    noise_ref,
    cell_ref,
    slab_ref,
    load_sem,
    out_sem,
    send_sem,
    recv_sem,
    tile_send,
    tile_recv,
):
    me = lax.axis_index("gx")
    planes, rows, lanes = pre.shape
    last = planes - 1
    chunk = rows // CHUNKS
    owned = noise_ref.shape[1]
    high = lax.rem(me + 1, count)
    low = lax.rem(me + count - 1, count)

    loads = [
        pltpu.make_async_copy(noise_hbm, noise_ref, load_sem.at[4]),
        pltpu.make_async_copy(cell_hbm, cell_ref, load_sem.at[5]),
        pltpu.make_async_copy(slab_hbm, slab_ref, load_sem.at[6]),
        pltpu.make_async_copy(direction_hbm, states.at[0], load_sem.at[0]),
        pltpu.make_async_copy(kappa_hbm, kappa, load_sem.at[1]),
        pltpu.make_async_copy(velocity_hbm, velocity, load_sem.at[2]),
        pltpu.make_async_copy(prior_hbm, prior, load_sem.at[3]),
    ]
    for load in loads:
        load.start()

    barrier = pltpu.get_barrier_semaphore()

    def greet(target):
        pl.semaphore_signal(
            barrier, inc=1, device_id={"gx": target}, device_id_type=pl.DeviceIdType.MESH
        )

    @pl.when(me > 0)
    def _():
        greet(low)

    @pl.when(me < count - 1)
    def _():
        greet(high)

    rounds = gather_rounds(count)

    def member(stride, radix, offset):
        digit = lax.rem(me // stride, radix)
        return me + (lax.rem(digit + offset, radix) - digit) * stride

    greeted = jnp.where((me == 0) | (me == count - 1), 1, 2)
    for stride, radix in rounds:
        for offset in range(1, radix):
            greet(member(stride, radix, offset))
        greeted = greeted + radix - 1

    for load in loads[:3]:
        load.wait()
    tiles[me, 0:STEPS, :] = noise_ref[...]
    tiles[me, STEPS : STEPS + 1, :] = cell_ref[...].astype(jnp.float32)
    tiles[me, STEPS + 1 : STEPS + 2, :] = slab_ref[...].astype(jnp.float32)
    tiles[me, STEPS + 2 :, :] = jnp.zeros((tiles.shape[1] - STEPS - 2, owned), jnp.float32)

    @pl.when(me == 0)
    def _():
        halo_low[...] = jnp.zeros_like(halo_low)

    @pl.when(me == count - 1)
    def _():
        halo_high[...] = jnp.zeros_like(halo_high)

    def span(part):
        return pl.ds(part * chunk, chunk)

    def to_high(source, slot, part):
        return pltpu.make_async_remote_copy(
            src_ref=source.at[span(part)],
            dst_ref=halo_low.at[slot, span(part)],
            send_sem=send_sem.at[0, slot, part],
            recv_sem=recv_sem.at[0, slot, part],
            device_id={"gx": high},
            device_id_type=pl.DeviceIdType.MESH,
        )

    def to_low(source, slot, part):
        return pltpu.make_async_remote_copy(
            src_ref=source.at[span(part)],
            dst_ref=halo_high.at[slot, span(part)],
            send_sem=send_sem.at[1, slot, part],
            recv_sem=recv_sem.at[1, slot, part],
            device_id={"gx": low},
            device_id_type=pl.DeviceIdType.MESH,
        )

    started = []

    def send(top, bottom, slot, part):
        started.append((top, bottom, slot, part))

        @pl.when(me < count - 1)
        def _():
            to_high(top, slot, part).start()

        @pl.when(me > 0)
        def _():
            to_low(bottom, slot, part).start()

    def arrive(slot, part):
        @pl.when(me > 0)
        def _():
            to_high(states.at[0, 0], slot, part).wait_recv()

        @pl.when(me < count - 1)
        def _():
            to_low(states.at[0, 0], slot, part).wait_recv()

    def settle(upper, arrived, finish, source, slot, part):
        copy = to_high if upper else to_low
        back = to_low if upper else to_high
        inside = me < count - 1 if upper else me > 0

        @pl.when(inside)
        def _():
            if arrived is not None:
                back(states.at[0, 0], arrived, part).wait_recv()
            finish(True)
            if source is not None:
                copy(source, slot, part).start()

        @pl.when(jnp.logical_not(inside))
        def _():
            finish(False)

    pl.semaphore_wait(barrier, greeted)
    loads[3].wait()
    for part in range(CHUNKS):
        send(states.at[0, last], states.at[0, 0], 0, part)

    def tile_copy(turn, offset, source):
        stride, radix = rounds[turn]
        block = tiles.at[pl.ds((source // stride) * stride, stride)]
        return pltpu.make_async_remote_copy(
            src_ref=block,
            dst_ref=block,
            send_sem=tile_send.at[turn, offset],
            recv_sem=tile_recv.at[turn, offset],
            device_id={"gx": member(stride, radix, offset)},
            device_id_type=pl.DeviceIdType.MESH,
        )

    def tile_start(turn):
        for offset in range(1, rounds[turn][1]):
            tile_copy(turn, offset, me).start()

    def tile_finish(turn):
        stride, radix = rounds[turn]
        for offset in range(1, radix):
            tile_copy(turn, offset, me).wait_send()
            tile_copy(turn, offset, member(stride, radix, radix - offset)).wait_recv()

    tile_start(0)

    row_at = lax.broadcasted_iota(jnp.int32, (rows, lanes), 0)
    lane_at = lax.broadcasted_iota(jnp.int32, (rows, lanes), 1)

    def next_row(value):
        return pltpu.roll(value, rows - 1, 0)

    def previous_row(value):
        return pltpu.roll(value, 1, 0)

    def next_lane(value):
        return pltpu.roll(value, lanes - 1, 1)

    def previous_lane(value):
        return pltpu.roll(value, 1, 1)

    loads[4].wait()
    loads[5].wait()
    for plane in range(planes):
        spread = kappa[plane]
        total = None
        edges = (None, None, row_at == rows - 1, row_at == 0, lane_at == lanes - 1, lane_at == 0)
        for column in range(3):
            speed = velocity[column, plane]
            for side in range(2):
                flow = jnp.maximum(-speed if side == 0 else speed, 0.0)
                piece = time_step * (spread + flow)
                total = piece if total is None else total + piece
                index = 2 * column + side
                edge = edges[index]
                coef[index, plane] = piece if edge is None else jnp.where(edge, 0.0, piece)
        centre[plane] = 1.0 - total

    def forward_local(step):
        for plane in range(planes):
            value = states[step, plane]
            result = centre[plane] * value
            if plane < last:
                result = result + coef[0, plane] * states[step, plane + 1]
            if plane > 0:
                result = result + coef[1, plane] * states[step, plane - 1]
            result = result + coef[2, plane] * next_row(value) + coef[3, plane] * previous_row(value)
            result = result + coef[4, plane] * next_lane(value) + coef[5, plane] * previous_lane(value)
            pre[plane] = result

    def prior_local(read, target, scale):
        for plane in range(planes):
            value = read(plane)
            result = (prior[plane] + 6.0) * value
            if plane < last:
                result = result - read(plane + 1)
            if plane > 0:
                result = result - read(plane - 1)
            result = result - jnp.where(row_at == rows - 1, 0.0, next_row(value))
            result = result - jnp.where(row_at == 0, 0.0, previous_row(value))
            result = result - jnp.where(lane_at == lanes - 1, 0.0, next_lane(value))
            result = result - jnp.where(lane_at == 0, 0.0, previous_lane(value))
            target[plane] = result

    prior_slot = 2 * STEPS

    def build_hot(first):
        def build(item, carry):
            tile = tiles.at[first + item]
            weight = tile[0:STEPS, :]
            cell = tile[STEPS : STEPS + 1, :].astype(jnp.int32)
            slab = tile[STEPS + 1 : STEPS + 2, :].astype(jnp.int32)
            row = jnp.where(slab == me, cell // lanes, -1)
            lane = cell % lanes
            at = pl.ds(pl.multiple_of(item * owned, owned), owned)
            tall = lax.broadcasted_iota(jnp.int32, (planes * rows, owned), 0)
            row_hot[:, at] = jnp.where(tall == row, 1.0, 0.0).astype(jnp.bfloat16)
            wide = lax.broadcasted_iota(jnp.int32, (lanes, owned), 0)
            here = wide == lane
            upper = weight.astype(jnp.bfloat16).astype(jnp.float32)
            lower = weight - upper
            for step in range(STEPS):
                lane_hot[step, 0:lanes, at] = jnp.where(here, upper[step : step + 1], 0.0).astype(jnp.bfloat16)
                lane_hot[step, lanes : 2 * lanes, at] = jnp.where(here, lower[step : step + 1], 0.0).astype(jnp.bfloat16)
            return carry

        lax.fori_loop(0, min(GROUP, count), build, 0)

    def add_density(step, first):
        both = lax.dot_general(
            row_hot[...],
            lane_hot[step],
            (((1,), (1,)), ((), ())),
            preferred_element_type=jnp.float32,
        )
        found = (both[:, :lanes] + both[:, lanes:]).reshape(planes, rows, lanes)
        if first:
            density[step] = found
        else:
            density[step] = density[step] + found

    def densities():
        build_hot(0)
        for step in range(STEPS):
            add_density(step, True)
        if count > GROUP:

            def more(block, carry):
                build_hot(block * GROUP)
                for step in range(STEPS):
                    add_density(step, False)
                return carry

            lax.fori_loop(1, count // GROUP, more, 0)

    for step in range(1, STEPS + 1):
        forward_local(step - 1)
        if step == 1:
            loads[6].wait()
            prior_local(lambda plane: states[0, plane], half, 1.0)
        if step == 2:
            half[0] = half[0] - halo_low[0]
            half[last] = half[last] - halo_high[0]
            for part in range(CHUNKS):
                send(half.at[last], half.at[0], prior_slot, part)
        if step == 2:
            tile_finish(0)
            if len(rounds) > 1:
                tile_start(1)
        if step == 3:
            for turn in range(1, len(rounds)):
                tile_finish(turn)
                if turn + 1 < len(rounds):
                    tile_start(turn + 1)
            if count > GROUP:
                densities()
            else:
                build_hot(0)
        if step == 4 and count <= GROUP:
            add_density(STEPS - 1, True)
        if step == 4:
            prior_local(lambda plane: half[plane], smooth, 1.0)
        for part in range(CHUNKS):
            at = span(part)
            if step < STEPS:
                started.append((states.at[step, last], states.at[step, 0], step, part))
            for plane in range(1, last):
                states[step, plane, at] = pre[plane, at]
            for upper in (True, False):
                plane = last if upper else 0

                def finish(near, plane=plane, upper=upper, at=at, step=step):
                    value = pre[plane, at]
                    if near:
                        halo = halo_high if upper else halo_low
                        side = 0 if upper else 1
                        value = value + coef[side, plane, at] * halo[step - 1, at]
                    states[step, plane, at] = value

                source = states.at[step, plane] if step < STEPS else None
                settle(upper, step - 1, finish, source, step, part)

    for order in range(STEPS):
        step = STEPS - order
        slot = STEPS + order
        if order == 0:
            pre[...] = density[step - 1] * states[step]
        for part in range(CHUNKS):
            at = span(part)
            started.append((sends.at[order, 0], sends.at[order, 1], slot, part))
            for plane in range(1, last):
                result[plane, at] = pre[plane, at]
            for upper in (True, False):
                plane = last if upper else 0

                def finish(near, plane=plane, upper=upper, at=at, step=step, order=order, slot=slot):
                    value = pre[plane, at]
                    if near and order > 0:
                        halo = halo_high if upper else halo_low
                        value = value + halo[slot - 1, at]
                    result[plane, at] = value
                    side = 0 if upper else 1
                    sends[order, side, at] = coef[side, plane, at] * value

                arrived = slot - 1 if order > 0 else None
                settle(upper, arrived, finish, sends.at[order, 0 if upper else 1], slot, part)
        if step > 1 and count <= GROUP:
            add_density(step - 2, True)
        for plane in range(planes):
            value = result[plane]
            total = centre[plane] * value
            if plane < last:
                total = total + coef[1, plane + 1] * result[plane + 1]
            if plane > 0:
                total = total + coef[0, plane - 1] * result[plane - 1]
            total = total + previous_row(coef[2, plane] * value) + next_row(coef[3, plane] * value)
            total = total + previous_lane(coef[4, plane] * value) + next_lane(coef[5, plane] * value)
            if step > 1:
                total = total + density[step - 2, plane] * states[step - 1, plane]
            else:
                total = total + prior_scale * smooth[plane]
            pre[plane] = total
        if order == 1:
            for part in range(CHUNKS):
                arrive(prior_slot, part)
            smooth[0] = smooth[0] - halo_low[prior_slot]
            smooth[last] = smooth[last] - halo_high[prior_slot]

    outs = []
    for part in range(CHUNKS):
        at = span(part)
        arrive(2 * STEPS - 1, part)
        for plane in range(planes):
            value = pre[plane, at]
            if plane == 0:
                value = value + halo_low[2 * STEPS - 1, at]
            if plane == last:
                value = value + halo_high[2 * STEPS - 1, at]
            result[plane, at] = value
        outs.append(pltpu.make_async_copy(result.at[:, at], out_hbm.at[:, at], out_sem.at[part]))
        outs[-1].start()

    @pl.when(me < count - 1)
    def _():
        for top, bottom, slot, part in started:
            to_high(top, slot, part).wait_send()

    @pl.when(me > 0)
    def _():
        for top, bottom, slot, part in started:
            to_low(bottom, slot, part).wait_send()

    for out in outs:
        out.wait()


def gather_rounds(count):
    rounds = []
    stride = 1
    while stride < count:
        radix = min(RADIX, count // stride)
        rounds.append((stride, radix))
        stride *= radix
    return rounds


def on_device(direction, kappa, velocity, prior_coef, noise_weight, sensor_cell, sensor_slab):
    count = lax.axis_size("gx")
    planes, rows, lanes = direction.shape
    owned = sensor_cell.shape[0]
    field = (planes, rows, lanes)
    slots = 2 * STEPS + 1
    group = min(GROUP, count) * owned
    hbm = pl.BlockSpec(memory_space=pltpu.HBM)
    vmem = pl.BlockSpec(memory_space=pltpu.VMEM)
    f32 = jnp.float32
    return pl.pallas_call(
        functools.partial(kernel, count),
        out_shape=jax.ShapeDtypeStruct(field, f32),
        in_specs=[hbm] * 7,
        out_specs=hbm,
        scratch_shapes=[
            pltpu.VMEM((STEPS + 1,) + field, f32),
            pltpu.VMEM(field, f32),
            pltpu.VMEM((3,) + field, f32),
            pltpu.VMEM(field, f32),
            pltpu.VMEM(field, f32),
            pltpu.VMEM((6,) + field, f32),
            pltpu.VMEM(field, f32),
            pltpu.VMEM(field, f32),
            pltpu.VMEM(field, f32),
            pltpu.VMEM((STEPS, 2, rows, lanes), f32),
            pltpu.VMEM((slots, rows, lanes), f32),
            pltpu.VMEM((slots, rows, lanes), f32),
            pltpu.VMEM((count, 8, owned), f32),
            pltpu.VMEM((planes * rows, group), jnp.bfloat16),
            pltpu.VMEM((STEPS, 2 * lanes, group), jnp.bfloat16),
            pltpu.VMEM((STEPS,) + field, f32),
            pltpu.VMEM(field, f32),
            pltpu.VMEM((STEPS, owned), f32),
            pltpu.VMEM((1, owned), jnp.int32),
            pltpu.VMEM((1, owned), jnp.int32),
            pltpu.SemaphoreType.DMA((7,)),
            pltpu.SemaphoreType.DMA((CHUNKS,)),
            pltpu.SemaphoreType.DMA((2, slots, CHUNKS)),
            pltpu.SemaphoreType.DMA((2, slots, CHUNKS)),
            pltpu.SemaphoreType.DMA((len(gather_rounds(count)), RADIX)),
            pltpu.SemaphoreType.DMA((len(gather_rounds(count)), RADIX)),
        ],
        compiler_params=pltpu.CompilerParams(
            collective_id=0, has_side_effects=True, vmem_limit_bytes=63 * 1024 * 1024
        ),
    )(
        direction,
        kappa,
        velocity,
        prior_coef,
        noise_weight,
        sensor_cell.reshape(1, owned),
        sensor_slab.reshape(1, owned),
    )


def solution(mesh):
    return jax.shard_map(
        on_device,
        mesh=mesh,
        in_specs=(
            P(("grp", "gx"), None, None),
            P(("grp", "gx"), None, None),
            P(None, ("grp", "gx"), None, None),
            P(("grp", "gx"), None, None),
            P(None, ("grp", "gx")),
            P(("grp", "gx")),
            P(("grp", "gx")),
        ),
        out_specs=P(("grp", "gx"), None, None),
        check_vma=False,
    )
```

```python
import functools

import jax
import jax.numpy as jnp
from jax import lax
from jax.experimental import pallas as pl
from jax.experimental.pallas import tpu as pltpu
from jax.sharding import PartitionSpec as P

STEPS = 4
CHUNKS = 4
GROUP = 16
RADIX = 4

time_step = 0.25
prior_scale = 0.01


def kernel(
    count,
    direction_hbm,
    kappa_hbm,
    velocity_hbm,
    prior_hbm,
    noise_hbm,
    cell_hbm,
    slab_hbm,
    out_hbm,
    states,
    kappa,
    velocity,
    prior,
    centre,
    coef,
    pre,
    smooth,
    half,
    sends,
    halo_low,
    halo_high,
    tiles,
    row_hot,
    lane_hot,
    density,
    result,
    noise_ref,
    cell_ref,
    slab_ref,
    load_sem,
    out_sem,
    send_sem,
    recv_sem,
    tile_send,
    tile_recv,
):
    me = lax.axis_index("gx")
    planes, rows, lanes = pre.shape
    last = planes - 1
    chunk = rows // CHUNKS
    owned = noise_ref.shape[1]
    high = lax.rem(me + 1, count)
    low = lax.rem(me + count - 1, count)

    loads = [
        pltpu.make_async_copy(noise_hbm, noise_ref, load_sem.at[4]),
        pltpu.make_async_copy(cell_hbm, cell_ref, load_sem.at[5]),
        pltpu.make_async_copy(slab_hbm, slab_ref, load_sem.at[6]),
        pltpu.make_async_copy(direction_hbm, states.at[0], load_sem.at[0]),
        pltpu.make_async_copy(kappa_hbm, kappa, load_sem.at[1]),
        pltpu.make_async_copy(velocity_hbm, velocity, load_sem.at[2]),
        pltpu.make_async_copy(prior_hbm, prior, load_sem.at[3]),
    ]
    for load in loads[3:4] + loads[:3] + loads[4:]:
        load.start()

    barrier = pltpu.get_barrier_semaphore()

    def greet(target):
        pl.semaphore_signal(
            barrier, inc=1, device_id={"gx": target}, device_id_type=pl.DeviceIdType.MESH
        )

    @pl.when(me > 0)
    def _():
        greet(low)

    @pl.when(me < count - 1)
    def _():
        greet(high)

    rounds = gather_rounds(count)

    def member(stride, radix, offset):
        digit = lax.rem(me // stride, radix)
        return me + (lax.rem(digit + offset, radix) - digit) * stride

    greeted = jnp.where((me == 0) | (me == count - 1), 1, 2)
    for stride, radix in rounds:
        for offset in range(1, radix):
            greet(member(stride, radix, offset))
        greeted = greeted + radix - 1

    for load in loads[:3]:
        load.wait()
    tiles[me, 0:STEPS, :] = noise_ref[...]
    tiles[me, STEPS : STEPS + 1, :] = cell_ref[...].astype(jnp.float32)
    tiles[me, STEPS + 1 : STEPS + 2, :] = slab_ref[...].astype(jnp.float32)
    tiles[me, STEPS + 2 :, :] = jnp.zeros((tiles.shape[1] - STEPS - 2, owned), jnp.float32)

    @pl.when(me == 0)
    def _():
        halo_low[...] = jnp.zeros_like(halo_low)

    @pl.when(me == count - 1)
    def _():
        halo_high[...] = jnp.zeros_like(halo_high)

    def span(part):
        return pl.ds(part * chunk, chunk)

    def to_high(source, slot, part):
        return pltpu.make_async_remote_copy(
            src_ref=source.at[span(part)],
            dst_ref=halo_low.at[slot, span(part)],
            send_sem=send_sem.at[0, slot, part],
            recv_sem=recv_sem.at[0, slot, part],
            device_id={"gx": high},
            device_id_type=pl.DeviceIdType.MESH,
        )

    def to_low(source, slot, part):
        return pltpu.make_async_remote_copy(
            src_ref=source.at[span(part)],
            dst_ref=halo_high.at[slot, span(part)],
            send_sem=send_sem.at[1, slot, part],
            recv_sem=recv_sem.at[1, slot, part],
            device_id={"gx": low},
            device_id_type=pl.DeviceIdType.MESH,
        )

    started = []

    def send(top, bottom, slot, part):
        started.append((top, bottom, slot, part))

        @pl.when(me < count - 1)
        def _():
            to_high(top, slot, part).start()

        @pl.when(me > 0)
        def _():
            to_low(bottom, slot, part).start()

    def arrive(slot, part):
        @pl.when(me > 0)
        def _():
            to_high(states.at[0, 0], slot, part).wait_recv()

        @pl.when(me < count - 1)
        def _():
            to_low(states.at[0, 0], slot, part).wait_recv()

    def settle(upper, arrived, finish, source, slot, part):
        copy = to_high if upper else to_low
        back = to_low if upper else to_high
        inside = me < count - 1 if upper else me > 0

        @pl.when(inside)
        def _():
            if arrived is not None:
                back(states.at[0, 0], arrived, part).wait_recv()
            finish(True)
            if source is not None:
                copy(source, slot, part).start()

        @pl.when(jnp.logical_not(inside))
        def _():
            finish(False)

    pl.semaphore_wait(barrier, greeted)
    loads[3].wait()
    for part in range(CHUNKS):
        send(states.at[0, last], states.at[0, 0], 0, part)

    def tile_copy(turn, offset, source):
        stride, radix = rounds[turn]
        block = tiles.at[pl.ds((source // stride) * stride, stride)]
        return pltpu.make_async_remote_copy(
            src_ref=block,
            dst_ref=block,
            send_sem=tile_send.at[turn, offset],
            recv_sem=tile_recv.at[turn, offset],
            device_id={"gx": member(stride, radix, offset)},
            device_id_type=pl.DeviceIdType.MESH,
        )

    def tile_start(turn):
        for offset in range(1, rounds[turn][1]):
            tile_copy(turn, offset, me).start()

    def tile_finish(turn):
        stride, radix = rounds[turn]
        for offset in range(1, radix):
            tile_copy(turn, offset, me).wait_send()
            tile_copy(turn, offset, member(stride, radix, radix - offset)).wait_recv()

    tile_start(0)

    row_at = lax.broadcasted_iota(jnp.int32, (rows, lanes), 0)
    lane_at = lax.broadcasted_iota(jnp.int32, (rows, lanes), 1)

    def next_row(value):
        return pltpu.roll(value, rows - 1, 0)

    def previous_row(value):
        return pltpu.roll(value, 1, 0)

    def next_lane(value):
        return pltpu.roll(value, lanes - 1, 1)

    def previous_lane(value):
        return pltpu.roll(value, 1, 1)

    loads[4].wait()
    loads[5].wait()
    for plane in range(planes):
        spread = kappa[plane]
        total = None
        edges = (None, None, row_at == rows - 1, row_at == 0, lane_at == lanes - 1, lane_at == 0)
        for column in range(3):
            speed = velocity[column, plane]
            for side in range(2):
                flow = jnp.maximum(-speed if side == 0 else speed, 0.0)
                piece = time_step * (spread + flow)
                total = piece if total is None else total + piece
                index = 2 * column + side
                edge = edges[index]
                coef[index, plane] = piece if edge is None else jnp.where(edge, 0.0, piece)
        centre[plane] = 1.0 - total

    def forward_local(step):
        for plane in range(planes):
            value = states[step, plane]
            result = centre[plane] * value
            if plane < last:
                result = result + coef[0, plane] * states[step, plane + 1]
            if plane > 0:
                result = result + coef[1, plane] * states[step, plane - 1]
            result = result + coef[2, plane] * next_row(value) + coef[3, plane] * previous_row(value)
            result = result + coef[4, plane] * next_lane(value) + coef[5, plane] * previous_lane(value)
            pre[plane] = result

    def prior_local(read, target, scale):
        for plane in range(planes):
            value = read(plane)
            result = (prior[plane] + 6.0) * value
            if plane < last:
                result = result - read(plane + 1)
            if plane > 0:
                result = result - read(plane - 1)
            result = result - jnp.where(row_at == rows - 1, 0.0, next_row(value))
            result = result - jnp.where(row_at == 0, 0.0, previous_row(value))
            result = result - jnp.where(lane_at == lanes - 1, 0.0, next_lane(value))
            result = result - jnp.where(lane_at == 0, 0.0, previous_lane(value))
            target[plane] = result

    prior_slot = 2 * STEPS

    def build_hot(first):
        def build(item, carry):
            tile = tiles.at[first + item]
            weight = tile[0:STEPS, :]
            cell = tile[STEPS : STEPS + 1, :].astype(jnp.int32)
            slab = tile[STEPS + 1 : STEPS + 2, :].astype(jnp.int32)
            row = jnp.where(slab == me, cell // lanes, -1)
            lane = cell % lanes
            at = pl.ds(pl.multiple_of(item * owned, owned), owned)
            tall = lax.broadcasted_iota(jnp.int32, (planes * rows, owned), 0)
            row_hot[:, at] = jnp.where(tall == row, 1.0, 0.0).astype(jnp.bfloat16)
            wide = lax.broadcasted_iota(jnp.int32, (lanes, owned), 0)
            here = wide == lane
            upper = weight.astype(jnp.bfloat16).astype(jnp.float32)
            lower = weight - upper
            for step in range(STEPS):
                lane_hot[step, 0:lanes, at] = jnp.where(here, upper[step : step + 1], 0.0).astype(jnp.bfloat16)
                lane_hot[step, lanes : 2 * lanes, at] = jnp.where(here, lower[step : step + 1], 0.0).astype(jnp.bfloat16)
            return carry

        lax.fori_loop(0, min(GROUP, count), build, 0)

    def add_density(step, first):
        both = lax.dot_general(
            row_hot[...],
            lane_hot[step],
            (((1,), (1,)), ((), ())),
            preferred_element_type=jnp.float32,
        )
        found = (both[:, :lanes] + both[:, lanes:]).reshape(planes, rows, lanes)
        if first:
            density[step] = found
        else:
            density[step] = density[step] + found

    def densities():
        build_hot(0)
        for step in range(STEPS):
            add_density(step, True)
        if count > GROUP:

            def more(block, carry):
                build_hot(block * GROUP)
                for step in range(STEPS):
                    add_density(step, False)
                return carry

            lax.fori_loop(1, count // GROUP, more, 0)

    for step in range(1, STEPS + 1):
        forward_local(step - 1)
        if step == 1:
            loads[6].wait()
            prior_local(lambda plane: states[0, plane], half, 1.0)
        if step == 2:
            half[0] = half[0] - halo_low[0]
            half[last] = half[last] - halo_high[0]
            for part in range(CHUNKS):
                send(half.at[last], half.at[0], prior_slot, part)
        if step == 2:
            tile_finish(0)
            if len(rounds) > 1:
                tile_start(1)
        if step == 3:
            for turn in range(1, len(rounds)):
                tile_finish(turn)
                if turn + 1 < len(rounds):
                    tile_start(turn + 1)
            if count > GROUP:
                densities()
            else:
                build_hot(0)
        if step == 4 and count <= GROUP:
            add_density(STEPS - 1, True)
        if step == 4:
            prior_local(lambda plane: half[plane], smooth, 1.0)
        for part in range(CHUNKS):
            at = span(part)
            if step < STEPS:
                started.append((states.at[step, last], states.at[step, 0], step, part))
            for plane in range(1, last):
                states[step, plane, at] = pre[plane, at]
            for upper in (True, False):
                plane = last if upper else 0

                def finish(near, plane=plane, upper=upper, at=at, step=step):
                    value = pre[plane, at]
                    if near:
                        halo = halo_high if upper else halo_low
                        side = 0 if upper else 1
                        value = value + coef[side, plane, at] * halo[step - 1, at]
                    states[step, plane, at] = value

                source = states.at[step, plane] if step < STEPS else None
                settle(upper, step - 1, finish, source, step, part)

    for order in range(STEPS):
        step = STEPS - order
        slot = STEPS + order
        if order == 0:
            pre[...] = density[step - 1] * states[step]
        for part in range(CHUNKS):
            at = span(part)
            started.append((sends.at[order, 0], sends.at[order, 1], slot, part))
            for plane in range(1, last):
                result[plane, at] = pre[plane, at]
            for upper in (True, False):
                plane = last if upper else 0

                def finish(near, plane=plane, upper=upper, at=at, step=step, order=order, slot=slot):
                    value = pre[plane, at]
                    if near and order > 0:
                        halo = halo_high if upper else halo_low
                        value = value + halo[slot - 1, at]
                    result[plane, at] = value
                    side = 0 if upper else 1
                    sends[order, side, at] = coef[side, plane, at] * value

                arrived = slot - 1 if order > 0 else None
                settle(upper, arrived, finish, sends.at[order, 0 if upper else 1], slot, part)
        if step > 1 and count <= GROUP:
            add_density(step - 2, True)
        for plane in range(planes):
            value = result[plane]
            total = centre[plane] * value
            if plane < last:
                total = total + coef[1, plane + 1] * result[plane + 1]
            if plane > 0:
                total = total + coef[0, plane - 1] * result[plane - 1]
            total = total + previous_row(coef[2, plane] * value) + next_row(coef[3, plane] * value)
            total = total + previous_lane(coef[4, plane] * value) + next_lane(coef[5, plane] * value)
            if step > 1:
                total = total + density[step - 2, plane] * states[step - 1, plane]
            else:
                total = total + prior_scale * smooth[plane]
            pre[plane] = total
        if order == 1:
            for part in range(CHUNKS):
                arrive(prior_slot, part)
            smooth[0] = smooth[0] - halo_low[prior_slot]
            smooth[last] = smooth[last] - halo_high[prior_slot]

    outs = []
    for part in range(CHUNKS):
        at = span(part)
        arrive(2 * STEPS - 1, part)
        for plane in range(planes):
            value = pre[plane, at]
            if plane == 0:
                value = value + halo_low[2 * STEPS - 1, at]
            if plane == last:
                value = value + halo_high[2 * STEPS - 1, at]
            result[plane, at] = value
        outs.append(pltpu.make_async_copy(result.at[:, at], out_hbm.at[:, at], out_sem.at[part]))
        outs[-1].start()

    @pl.when(me < count - 1)
    def _():
        for top, bottom, slot, part in started:
            to_high(top, slot, part).wait_send()

    @pl.when(me > 0)
    def _():
        for top, bottom, slot, part in started:
            to_low(bottom, slot, part).wait_send()

    for out in outs:
        out.wait()


def gather_rounds(count):
    rounds = []
    stride = 1
    while stride < count:
        radix = min(RADIX, count // stride)
        rounds.append((stride, radix))
        stride *= radix
    return rounds


def on_device(direction, kappa, velocity, prior_coef, noise_weight, sensor_cell, sensor_slab):
    count = lax.axis_size("gx")
    planes, rows, lanes = direction.shape
    owned = sensor_cell.shape[0]
    field = (planes, rows, lanes)
    slots = 2 * STEPS + 1
    group = min(GROUP, count) * owned
    hbm = pl.BlockSpec(memory_space=pltpu.HBM)
    vmem = pl.BlockSpec(memory_space=pltpu.VMEM)
    f32 = jnp.float32
    return pl.pallas_call(
        functools.partial(kernel, count),
        out_shape=jax.ShapeDtypeStruct(field, f32),
        in_specs=[hbm] * 7,
        out_specs=hbm,
        scratch_shapes=[
            pltpu.VMEM((STEPS + 1,) + field, f32),
            pltpu.VMEM(field, f32),
            pltpu.VMEM((3,) + field, f32),
            pltpu.VMEM(field, f32),
            pltpu.VMEM(field, f32),
            pltpu.VMEM((6,) + field, f32),
            pltpu.VMEM(field, f32),
            pltpu.VMEM(field, f32),
            pltpu.VMEM(field, f32),
            pltpu.VMEM((STEPS, 2, rows, lanes), f32),
            pltpu.VMEM((slots, rows, lanes), f32),
            pltpu.VMEM((slots, rows, lanes), f32),
            pltpu.VMEM((count, 8, owned), f32),
            pltpu.VMEM((planes * rows, group), jnp.bfloat16),
            pltpu.VMEM((STEPS, 2 * lanes, group), jnp.bfloat16),
            pltpu.VMEM((STEPS,) + field, f32),
            pltpu.VMEM(field, f32),
            pltpu.VMEM((STEPS, owned), f32),
            pltpu.VMEM((1, owned), jnp.int32),
            pltpu.VMEM((1, owned), jnp.int32),
            pltpu.SemaphoreType.DMA((7,)),
            pltpu.SemaphoreType.DMA((CHUNKS,)),
            pltpu.SemaphoreType.DMA((2, slots, CHUNKS)),
            pltpu.SemaphoreType.DMA((2, slots, CHUNKS)),
            pltpu.SemaphoreType.DMA((len(gather_rounds(count)), RADIX)),
            pltpu.SemaphoreType.DMA((len(gather_rounds(count)), RADIX)),
        ],
        compiler_params=pltpu.CompilerParams(
            collective_id=0, has_side_effects=True, vmem_limit_bytes=63 * 1024 * 1024
        ),
    )(
        direction,
        kappa,
        velocity,
        prior_coef,
        noise_weight,
        sensor_cell.reshape(1, owned),
        sensor_slab.reshape(1, owned),
    )


def solution(mesh):
    return jax.shard_map(
        on_device,
        mesh=mesh,
        in_specs=(
            P(("grp", "gx"), None, None),
            P(("grp", "gx"), None, None),
            P(None, ("grp", "gx"), None, None),
            P(("grp", "gx"), None, None),
            P(None, ("grp", "gx")),
            P(("grp", "gx")),
            P(("grp", "gx")),
        ),
        out_specs=P(("grp", "gx"), None, None),
        check_vma=False,
    )
```
